32 devices in a mesh: groups: 2 (over y), tm: 8 (over z, x), space: 2 (over core).
Axes of the slice: x: 2, y: 2, z: 4, core: 2. Of those that a mesh axis runs over, the one named last changes fastest.
Arguments:
- initial: float32 [16, 1024], P(('groups', 'space')), parts along dimension 0, may hold values from -6 to 6
- forcing: float32 [16, 8, 1024], P(('groups', 'tm'), 'space'), parts along dimension 0, may hold values from -1.25 to 1.25
- velocity_x: float32 [16, 1024], P(('groups', 'space')), parts along dimension 0, may hold values from -0.4 to 0.4
- velocity_y: float32 [16, 1024], P(('groups', 'space')), parts along dimension 0, may hold values from -0.4 to 0.4
- cotangent: float32 [16, 8, 1024], P(('groups', 'tm'), 'space'), parts along dimension 0, may hold values from -0.1875 to 0.1875
- w_first: float32 [9, 64, 3], replicated, may hold values from -1.25 to 1.25
- bias_first: float32 [64], replicated, may hold values from -3 to 3
- w_middle: float32 [9, 64, 64], replicated, may hold values from -0.25 to 0.25
- bias_middle: float32 [64], replicated, may hold values from -3 to 3
- w_last: float32 [9, 2, 64], replicated, may hold values from -0.25 to 0.25
- bias_last: float32 [2], replicated, may hold values from -6 to 6
Outputs:
- grad_w_first: float32 [18, 64, 3], P('groups'), parts along dimension 0
- grad_bias_first: float32 [128], P('groups'), parts along dimension 0
- grad_w_middle: float32 [18, 64, 64], P('groups'), parts along dimension 0
- grad_bias_middle: float32 [128], P('groups'), parts along dimension 0
- grad_w_last: float32 [18, 2, 64], P('groups'), parts along dimension 0
- grad_bias_last: float32 [4], P('groups'), parts along dimension 0
The draws below stay inside these ranges and needn't reach their ends.
There are 2 independent parts, one for each index of `groups`. The reference program is written for one: setup_inputs(seed, part) draws one part's arguments, and reference() takes and returns one part's arrays. A program takes and returns all parts, laid end to end along the dimension named above; an argument that names none is the same for every part. Nothing has to cross between parts.
All inputs are finite; a program needn't handle non-finite values.
Results may differ from the reference program's by a relative error of at most 0.0002.
Values sent between devices are 32-bit elements; how exact they have to be, the bound alone decides.
A program may use at most 64 MiB of HBM per device.

```python
import jax
import jax.numpy as jnp
from jax import lax

NX = 1024
CH = 64
FSTEPS = 4
SLICES = 8
NY = 8


def block_levels(rng, dims, cuts, low, largest):
    def one(axis_at, blocks):
        heights = jax.random.uniform(jax.random.fold_in(jax.random.fold_in(rng, 6), axis_at), (blocks,), jnp.float32, low / len(cuts), largest / len(cuts))
        return jnp.repeat(jnp.exp(heights), dims[axis_at] // blocks).reshape((-1,) + (1,) * (len(dims) - axis_at - 1))

    level = one(*cuts[0])
    for cut in cuts[1:]:
        level = level * one(*cut)
    return level


def noise(key, extent, width, most, cuts=(), dtype=jnp.bfloat16):
    gain = block_levels(key, extent, cuts, -0.22, 0.18) if cuts else 1.0
    values = jax.random.normal(key, extent, jnp.float32) * width * gain
    return jnp.minimum(jnp.maximum(values, -most), most).astype(dtype)


def setup_inputs(seed: int = 0, part: int = 0) -> dict:
    keys = jax.random.split(jax.random.key(seed), 12)
    part_keys = jax.random.split(jax.random.fold_in(keys[11], part), 12)
    initial = noise(part_keys[0], (NY, NX), 1.0, 6.0, ((0, 2),), jnp.float32)
    forcing = noise(part_keys[1], (SLICES, NY, NX), 0.2, 1.25, ((0, 8), (1, 2)), jnp.float32)
    velocity_x = jnp.clip(jax.random.uniform(part_keys[2], (NY, NX), jnp.float32, -0.4, 0.4) * block_levels(part_keys[2], (NY, NX), ((0, 2),), -0.4, 0.0), -0.4, 0.4)
    velocity_y = jnp.clip(jax.random.uniform(part_keys[3], (NY, NX), jnp.float32, -0.4, 0.4) * block_levels(part_keys[3], (NY, NX), ((0, 2),), -0.4, 0.0), -0.4, 0.4)
    cotangent = noise(part_keys[4], (SLICES, NY, NX), (0.25 * SLICES / (SLICES * NY * NX // 16) ** 0.5), 0.1875, ((0, 8), (1, 2)), jnp.float32)
    w_first = noise(keys[5], (9, CH, 3), 27 ** -0.5, 1.25, (), jnp.float32)
    bias_first = noise(keys[6], (CH,), 0.5, 3.0, (), jnp.float32)
    w_middle = noise(keys[7], (9, CH, CH), (9 * CH) ** -0.5, 0.25, (), jnp.float32)
    bias_middle = noise(keys[8], (CH,), 0.5, 3.0, (), jnp.float32)
    w_last = noise(keys[9], (9, 2, CH), (9 * CH) ** -0.5, 0.25, (), jnp.float32)
    bias_last = noise(keys[10], (2,), 1.0, 6.0, (), jnp.float32)
    return dict(initial=initial, forcing=forcing, velocity_x=velocity_x, velocity_y=velocity_y, cotangent=cotangent, w_first=w_first, bias_first=bias_first, w_middle=w_middle, bias_middle=bias_middle, w_last=w_last, bias_last=bias_last)


time_step = 0.5
viscosity = 0.2

def restrict(field):
    shape = field.shape
    blocks = field.reshape(shape[:-2] + (shape[-2] // 4, 4, shape[-1] // 4, 4))
    return blocks.mean(axis=(-3, -1))

def prolong(coarse):
    return jnp.repeat(jnp.repeat(coarse, 4, axis=-2), 4, axis=-1)

def conv_periodic(inputs, kernel, offset_bias):
    padded = jnp.pad(inputs, ((0, 0), (1, 1), (1, 1)), mode='wrap')
    rows_here = inputs.shape[1]
    cols_here = inputs.shape[2]
    output = jnp.zeros((kernel.shape[1], rows_here, cols_here), jnp.float32) + offset_bias[:, None, None]
    for tap_row in range(3):
        for tap_col in range(3):
            window = padded[:, tap_row:tap_row + rows_here, tap_col:tap_col + cols_here]
            output = output + jnp.einsum('oc,crw->orw', kernel[3 * tap_row + tap_col], window, precision=lax.Precision.HIGHEST)
    return output

def network(forcing_slice, velocity_x, velocity_y, params):
    w_first, bias_first, w_middle, bias_middle, w_last, bias_last = params
    inputs = jnp.stack([restrict(forcing_slice), restrict(velocity_x), restrict(velocity_y)])
    hidden_one = jnp.tanh(conv_periodic(inputs, w_first, bias_first))
    hidden_two = jnp.tanh(conv_periodic(hidden_one, w_middle, bias_middle))
    output = conv_periodic(hidden_two, w_last, bias_last)
    gate = jax.nn.sigmoid(output[0])
    return (jnp.exp(-(3.0 / SLICES) * gate), output[1] / SLICES)

def fine_step(field, forcing, velocity_x, velocity_y):
    upper_row = jnp.roll(field, -1, axis=-2)
    lower_row = jnp.roll(field, 1, axis=-2)
    east_col = jnp.roll(field, -1, axis=-1)
    west_col = jnp.roll(field, 1, axis=-1)
    laplace = upper_row + lower_row + east_col + west_col - 4.0 * field
    return field + time_step * (viscosity * laplace - velocity_x * (east_col - west_col) * 0.5 - velocity_y * (upper_row - lower_row) * 0.5 + forcing)

def fine_solve(states, forcing, velocity_x, velocity_y):
    for repeat_index in range(FSTEPS):
        states = fine_step(states, forcing, velocity_x, velocity_y)
    return states

def reference(initial, forcing, velocity_x, velocity_y, cotangent, w_first, bias_first, w_middle, bias_middle, w_last, bias_last):

    def loss(params):
        decay, source = jax.vmap(network, in_axes=(0, None, None, None))(forcing, velocity_x, velocity_y, params)

        def sweep_first(state, item):
            decay_one, source_one = item
            return (prolong(decay_one * restrict(state) + source_one), state)
        unused, starts_zero = lax.scan(sweep_first, initial, (decay, source))
        fine_zero = fine_solve(starts_zero, forcing, velocity_x, velocity_y)

        def sweep_next(state, item):
            decay_one, source_one, fine_one, older = item
            newer = prolong(decay_one * restrict(state) + source_one) + fine_one - prolong(decay_one * restrict(older) + source_one)
            return (newer, (state, newer))
        unused, (starts_one, ends_one) = lax.scan(sweep_next, initial, (decay, source, fine_zero, starts_zero))
        fine_one = fine_solve(starts_one, forcing, velocity_x, velocity_y)
        unused, (starts_two, ends_two) = lax.scan(sweep_next, initial, (decay, source, fine_one, starts_one))
        return jnp.sum(cotangent * ends_two)
    grads = jax.grad(loss)((w_first, bias_first, w_middle, bias_middle, w_last, bias_last))
    return (grads[0], grads[1], grads[2], grads[3], grads[4], grads[5])
```

```python
import functools

import jax
import jax.numpy as jnp
from jax import lax
from jax.experimental import pallas as pl
from jax.experimental.pallas import tpu as pltpu
from jax.sharding import PartitionSpec as P

f32, bf16 = jnp.float32, jnp.bfloat16
MESH = pl.DeviceIdType.MESH
CB = 256
CW = 512
OWNERS = 8


def roll(x, shift, axis):
    return pltpu.roll(x, shift % x.shape[axis], axis)


def iota(shape, dim):
    return lax.broadcasted_iota(jnp.int32, shape, dim)


def split(x):
    high = x.astype(bf16)
    return high, (x - high.astype(f32)).astype(bf16)


def dot(a, b, dims):
    return lax.dot_general(a, b, (dims, ((), ())), preferred_element_type=f32)


def dot3(a, b, dims):
    (ah, al), (bh, bl) = a, b
    return dot(ah, bh, dims) + (dot(ah, bl, dims) + dot(al, bh, dims))


NN = ((1,), (0,))
NT = ((1,), (1,))


def east(f):
    return jnp.concatenate([f[..., CB:], roll(f[..., :CB], -1, f.ndim - 1)], axis=-1)


def west(f):
    return jnp.concatenate([roll(f[..., 3 * CB :], 1, f.ndim - 1), f[..., : 3 * CB]], axis=-1)


def step(f, co):
    up, dn, ea, we = co
    ax = f.ndim - 2
    return (0.6 * f + (up * roll(f, -1, ax) + dn * roll(f, 1, ax))) + (ea * east(f) + we * west(f))


def step_t(f, co):
    up, dn, ea, we = co
    ax = f.ndim - 2
    return (0.6 * f + (roll(up * f, 1, ax) + roll(dn * f, -1, ax))) + (west(ea * f) + east(we * f))


def restrict(f):
    z = (f[:, :CB] + f[:, CB : 2 * CB]) + (f[:, 2 * CB : 3 * CB] + f[:, 3 * CB :])
    z = z + roll(z, -1, 0)
    z = (z + roll(z, -2, 0)) * (1.0 / 16.0)
    return jnp.concatenate([z[0:1], z[4:5]], axis=1)


def swap(x):
    return jnp.concatenate([x[:, CB:], x[:, :CB]], axis=1)


def col(x, d):
    if d == 0:
        return x
    return jnp.concatenate([roll(x[:, :CB], -d, 1), roll(x[:, CB:], -d, 1)], axis=1)


def stack(x):
    return jnp.concatenate([col(x, -1), x, col(x, 1)], axis=0)


def apply_k(x, ca, cb):
    reach = len(ca) // 2
    y = swap(x)
    out = None
    for d in range(-reach, reach + 1):
        term = ca[d + reach] * col(x, d) + cb[d + reach] * col(y, d)
        out = term if out is None else out + term
    return out


def apply_kt(x, ca, cb):
    reach = len(ca) // 2
    out = None
    for d in range(-reach, reach + 1):
        term = col(ca[d + reach] * x + swap(cb[d + reach] * x), -d)
        out = term if out is None else out + term
    return out


def probes(co):
    b = iota((8, 4 * CB), 1) % CB
    band = iota((8, 4 * CB), 0) // 4
    lane = iota((1, CW), 1)
    j, first = lane % CB, lane < CB

    def pair(fields):
        r0, r1 = restrict(fields[0]), restrict(fields[1])
        return jnp.where(first, r0, r1), jnp.where(first, r1, r0)

    c4 = [[jnp.zeros((1, CW), f32) for _ in range(3)] for _ in range(2)]
    c8 = [[jnp.zeros((1, CW), f32) for _ in range(5)] for _ in range(2)]

    def put(c, values, color, period):
        reach = len(c[0]) // 2
        for kind in range(2):
            for d in range(-reach, reach + 1):
                here = (j + (d + period)) % period == color
                c[kind][d + reach] = jnp.where(here, values[kind], c[kind][d + reach])

    for p in range(4):
        fields = [jnp.where((b % 4 == p) & (band == i), 1.0, 0.0).astype(f32) for i in range(2)]
        for _ in range(4):
            fields = [step(f, co) for f in fields]
        put(c4, pair(fields), p, 4)
        for p8 in (p, p + 4):
            near = (b + (9 - p8)) % 8 <= 2
            wide = [jnp.where(near, f, 0.0) for f in fields]
            for _ in range(4):
                wide = [step(f, co) for f in wide]
            put(c8, pair(wide), p8, 8)
    return c4, c8


def down(x, first):
    row = iota(x.shape, 0)
    return jnp.where(row == 0, first, roll(x, 1, 0))


def upward(x):
    row = iota(x.shape, 0)
    return jnp.where(row == x.shape[0] - 1, 0.0, roll(x, -1, 0))


def scanner(d, reverse):
    n = d.shape[0]
    row = iota(d.shape, 0)
    levels, k = [], 1
    while k < n:
        shift, ok = (-k, row < n - k) if reverse else (k, row >= k)
        levels.append((k, jnp.where(ok, d, 0.0)))
        d = d * jnp.where(ok, roll(d, shift, 0), 1.0)
        k *= 2

    def run(u):
        for k, factor in levels:
            u = u + factor * roll(u, -k if reverse else k, 0)
        return u

    return run


def sweeps(parts, r_init, a4_init, a8_init, k4, k8):
    d, src, s1, s2, q0, q1, q2 = parts
    row = iota(d.shape, 0)
    forward, backward = scanner(d, False), scanner(d, True)
    c0_next = forward(src + jnp.where(row == 0, d * r_init, 0.0))
    c0 = down(c0_next, r_init)
    rf0 = jnp.where(row == 0, a4_init, apply_k(c0, *k4)) + s1
    e1_next = forward(rf0 - c0_next)
    e1 = down(e1_next, 0.0)
    de1 = d * e1
    w = apply_k(de1, *k4) + jnp.where(row == 0, a8_init, apply_k(c0, *k8)) + s2
    rf1 = down(w, a4_init) + s1
    e2 = down(forward(rf1 - rf0 - de1), 0.0)

    lam = upward(backward(d * q0))
    r2 = q0 + lam
    r1 = upward(backward(q1 + apply_kt(lam, *k4) - d * r2))
    bb = q2 + apply_kt(lam, *k8) + apply_kt(d * (r1 - r2), *k4)
    r0 = upward(backward(upward(bb) - d * r1))
    return c0, e1, e2, r2, r1, r0


def column(row_vector):
    n = row_vector.shape[1]
    eye = iota((n, n), 0) == iota((n, n), 1)
    return jnp.sum(jnp.where(eye, row_vector, 0.0), axis=1, keepdims=True)


def kernel(
    count,
    initial, forcing, vel_x, vel_y, cot,
    w_first, b_first, w_middle, b_middle, w_last, b_last,
    g_first, gb_first, g_middle, gb_middle, g_last, gb_last,
    comb, gat, pack, part, full,
    s0, r0sem, s1sem, r1sem, s2sem, r2sem, s3a, s3b, r3sem,
):
    me, core = lax.axis_index("tm"), lax.axis_index("space")
    other = 1 - core

    def peers(body):
        if count <= 8:
            for d in range(1, count):
                body(lax.rem(me + d, count))
        else:
            lax.fori_loop(1, count, lambda d, c: (body(lax.rem(me + d, count)), c)[1], 0)

    barrier = pltpu.get_barrier_semaphore()

    def greet(t, c):
        pl.semaphore_signal(barrier, inc=1, device_id={"tm": t, "space": c}, device_id_type=MESH)

    greet(me, other)
    peers(lambda t: (greet(t, core), greet(t, other)))

    def remote(src, dst, send, recv, t, c):
        return pltpu.make_async_remote_copy(
            src_ref=src, dst_ref=dst, send_sem=send, recv_sem=recv,
            device_id={"tm": t, "space": c}, device_id_type=MESH,
        )

    def drain(ref, sem):
        pltpu.make_async_copy(ref, ref, sem).wait()

    mine = comb.at[core]
    mine[0] = forcing[0]
    mine[1] = vel_x[...]
    mine[2] = vel_y[...]
    mine[3] = initial[...]
    mine[4] = cot[0]

    mid_a = [w_middle[3 + q] for q in range(3)]
    mid_b = [w_middle[q] + w_middle[6 + q] for q in range(3)]
    mid = split(jnp.concatenate(
        [jnp.concatenate(mid_a, axis=1), jnp.concatenate(mid_b, axis=1)], axis=0))
    mid_t = split(jnp.concatenate(
        [jnp.concatenate([a, b], axis=1) for a, b in zip(mid_a, mid_b)], axis=0).T)
    fst_a = [w_first[3 + q] for q in range(3)]
    fst_b = [w_first[q] + w_first[6 + q] for q in range(3)]
    lst_a = [w_last[3 + q] for q in range(3)]
    lst_b = [w_last[q] + w_last[6 + q] for q in range(3)]
    lst = split(jnp.concatenate(
        [jnp.concatenate(lst_a, axis=1), jnp.concatenate(lst_b, axis=1),
         jnp.zeros((12, 192), f32)], axis=0))
    lst_t = jnp.concatenate(lst_a + lst_b + [jnp.zeros((4, 64), f32)], axis=0).T
    bias1, bias2 = column(b_first[...]), column(b_middle[...])
    src_lane, dst_lane = iota((CW, CW), 0), iota((CW, CW), 1)
    order = jnp.where(src_lane == 4 * (dst_lane % 128) + dst_lane // 128, 1.0, 0.0).astype(bf16)

    pl.semaphore_wait(barrier, 2 * count - 1)
    bands = remote(mine, mine, s0, r0sem, me, other)
    bands.start()
    bands.wait()

    rows = []
    for k in range(5):
        x = jnp.concatenate([comb[0, k], comb[1, k]], axis=0)
        rows += [x[:, :CW], x[:, CW:]]
    x = jnp.concatenate(rows, axis=0)
    high, rest = split(x)
    low = (x - high.astype(f32) - rest.astype(f32)).astype(bf16)
    y = dot(jnp.concatenate([high, rest, low], axis=0), order, NN)
    y = (y[0:80] + y[80:160]) + y[160:240]
    fields = []
    for k in range(5):
        pieces = []
        for s in range(4):
            for h in range(2):
                pieces.append(y[16 * k + 8 * h : 16 * k + 8 * h + 8, 128 * s : 128 * s + 128])
        fields.append(jnp.concatenate(pieces, axis=1))
    force, vx, vy, start, weight = fields

    inputs = [restrict(force), restrict(vx), restrict(vy)]
    pre = jnp.broadcast_to(bias1, (64, CW))
    shifted = [[col(inputs[c], q - 1) for c in range(3)] for q in range(3)]
    for q in range(3):
        for c in range(3):
            v = shifted[q][c]
            pre = pre + (fst_a[q][:, c : c + 1] * v + fst_b[q][:, c : c + 1] * swap(v))
    hidden1 = jnp.tanh(pre)
    stack1 = split(stack(hidden1))
    z = dot3(mid, stack1, NN)
    hidden2 = jnp.tanh(z[:64] + swap(z[64:]) + bias2)
    stack2f = stack(hidden2)
    z = dot3(lst, split(stack2f), NN)
    out = z[0:2] + swap(z[2:4])
    rate = 3.0 / count
    gate = 1.0 / (1.0 + jnp.exp(-(out[0:1] + b_last[0:1, 0:1])))
    decay = jnp.exp(-rate * gate)
    source = (out[1:2] + b_last[0:1, 1:2]) * (1.0 / count)

    co = (0.1 - 0.25 * vy, 0.1 + 0.25 * vy, 0.1 - 0.25 * vx, 0.1 + 0.25 * vx)
    half = 0.5 * force
    sf, av, tv = half, start, weight
    for _ in range(3):
        sf = step(sf, co) + half
    s1 = restrict(sf)
    q0 = restrict(weight)
    for _ in range(4):
        sf, tv = step(sf, co), step_t(tv, co)
    s2, q1 = restrict(sf), restrict(tv)
    for _ in range(4):
        tv = step_t(tv, co)
    q2 = restrict(tv)

    gat[me] = jnp.concatenate(
        [decay, source, s1, s2, q0, q1, q2, jnp.zeros((1, CW), f32)], axis=0)
    peers(lambda t: remote(gat.at[me], gat.at[me], s1sem, r1sem, t, core).start())

    r_init = restrict(start)
    for _ in range(4):
        av = step(av, co)
    a4_init = restrict(av)
    for _ in range(4):
        av = step(av, co)
    a8_init = restrict(av)
    k4, k8 = probes(co)

    drain(gat.at[pl.ds(0, count - 1)], r1sem)
    parts = [gat[:, k, :] for k in range(7)]
    results = sweeps(parts, r_init, a4_init, a8_init, k4, k8)
    here = iota((count, CW), 0) == me
    c0, e1, e2, r2, r1, r0 = [
        jnp.sum(jnp.where(here, v, 0.0), axis=0, keepdims=True) for v in results]
    g_decay = 16.0 * (r2 * e2 + r1 * e1 + r0 * c0)
    go = [g_decay * decay * (-rate) * gate * (1.0 - gate), r0 * (16.0 / count)]

    own = core == 0

    def kind(v):
        return jnp.where(own, v, swap(v))

    grad2 = jnp.zeros((64, CW), f32)
    for q in range(3):
        for o in range(2):
            v = col(go[o], 1 - q)
            at = 2 * q + o
            grad2 = grad2 + (lst_t[:, at : at + 1] * v + lst_t[:, 6 + at : 7 + at] * swap(v))
    grad2 = grad2 * (1.0 - hidden2 * hidden2)
    z = dot3(mid_t, split(jnp.concatenate([col(grad2, 1), grad2, col(grad2, -1)], axis=0)), NN)
    grad1 = (z[:64] + swap(z[64:])) * (1.0 - hidden1 * hidden1)
    gmid = dot3(split(kind(grad2)), stack1, NT)

    def lane_sum(v):
        return jnp.sum(v, axis=1, keepdims=True)

    grad1k = kind(grad1)
    gok = [kind(v) for v in go]
    columns = [lane_sum(grad1k * shifted[q][c]) for q in range(3) for c in range(3)]
    columns += [lane_sum(grad1), lane_sum(grad2)]
    columns += [
        lane_sum(gok[o] * stack2f[64 * q : 64 * q + 64]) for q in range(3) for o in range(2)]
    columns += [jnp.broadcast_to(lane_sum(v), (64, 1)) for v in go]
    lane = iota((64, 64), 1)
    tail = jnp.zeros((64, 64), f32)
    for k, v in enumerate(columns):
        tail = jnp.where(lane == k, v, tail)
    pack[...] = jnp.concatenate([gmid, tail], axis=1)

    def to_owner(t):
        return remote(pack.at[pl.ds(8 * t, 8)], part.at[me], s2sem, r2sem, t, core)

    def spread(body):
        if count == OWNERS:
            body()
        else:
            pl.when(me < OWNERS)(body)

    if count == OWNERS:
        peers(lambda t: to_owner(t).start())
        drain(part.at[pl.ds(0, count - 1)], r2sem)
    else:
        for t in range(OWNERS):
            pl.when(me != t)(lambda t=t: to_owner(t).start())
        spread(lambda: drain(part.at[pl.ds(0, count - 1)], r2sem))

    def publish():
        at = pl.multiple_of(8 * me, 8)
        part[me] = pack[pl.ds(at, 8)]
        total = part[0]
        if count <= 8:
            for t in range(1, count):
                total = total + part[t]
        else:
            total = lax.fori_loop(1, count, lambda t, acc: acc + part[t], total)
        shard = full.at[pl.ds(pl.multiple_of(64 * core + 8 * me, 8), 8)]
        shard[...] = total
        remote(shard, shard, s3b, r3sem, me, other).start()
        peers(lambda t: (remote(shard, shard, s3a, r3sem, t, core).start(),
                         remote(shard, shard, s3b, r3sem, t, other).start()))

    spread(publish)
    if count == OWNERS:
        drain(full.at[pl.ds(0, 120)], r3sem)
    else:
        pl.when(me < OWNERS)(lambda: drain(full.at[pl.ds(0, 120)], r3sem))
        pl.when(me >= OWNERS)(lambda: drain(full, r3sem))

    for k in range(2):
        taps = (1,) if k == 0 else (0, 2)
        grads = full[64 * k : 64 * k + 64, :]
        turned = grads[:, 128:].T
        for q in range(3):
            for p in taps:
                g_middle[3 * p + q] = grads[:, 64 * q : 64 * q + 64]
                g_first[3 * p + q] = grads[:, 192 + 3 * q : 195 + 3 * q]
                g_last[3 * p + q] = turned[75 + 2 * q : 77 + 2 * q, :]
        if k == 0:
            gb_first[...] = turned[73:74, :]
            gb_middle[...] = turned[74:75, :]
            gb_last[...] = grads[0:1, 209:211]

    drain(gat.at[pl.ds(0, count - 1)], s1sem)
    if count == OWNERS:
        drain(part.at[pl.ds(0, count - 1)], s2sem)
    else:
        pl.when(me < OWNERS)(lambda: drain(pack.at[pl.ds(0, 56)], s2sem))
        pl.when(me >= OWNERS)(lambda: drain(pack, s2sem))

    def sent():
        drain(part.at[pl.ds(0, count - 1)], s3a)
        drain(part, s3b)

    spread(sent)


def per_device(count, *args):
    initial, forcing, vx, vy, cot, w1, b1, w2, b2, w3, b3 = args
    vmem = pl.BlockSpec(memory_space=pltpu.VMEM)
    dma = pltpu.SemaphoreType.DMA
    outs = pl.pallas_call(
        functools.partial(kernel, count),
        out_shape=[
            jax.ShapeDtypeStruct(s, f32)
            for s in ((9, 64, 3), (1, 64), (9, 64, 64), (1, 64), (9, 2, 64), (1, 2))],
        in_specs=[vmem] * 11,
        out_specs=[vmem] * 6,
        scratch_shapes=[
            pltpu.VMEM((2, 5, 4, 1024), f32),
            pltpu.VMEM((count, 8, CW), f32),
            pltpu.VMEM((64, 256), f32),
            pltpu.VMEM((count, 8, 256), f32),
            pltpu.VMEM((128, 256), f32),
        ] + [dma] * 9,
        compiler_params=pltpu.CompilerParams(
            collective_id=0, has_side_effects=True, vmem_limit_bytes=40 * 1024 * 1024),
    )(initial, forcing, vx, vy, cot, w1, b1.reshape(1, 64), w2, b2.reshape(1, 64), w3,
      b3.reshape(1, 2))
    return (outs[0], outs[1].reshape(64), outs[2], outs[3].reshape(64), outs[4],
            outs[5].reshape(2))


def solution(mesh):
    band, piece = P(("groups", "space"), None), P(("groups", "tm"), "space", None)
    return jax.shard_map(
        functools.partial(per_device, mesh.shape["tm"]),
        mesh=mesh,
        in_specs=(band, piece, band, band, piece) + (P(),) * 6,
        out_specs=(
            P("groups", None, None), P("groups"), P("groups", None, None), P("groups"),
            P("groups", None, None), P("groups"),
        ),
        check_vma=False,
    )
```

```python
import functools

import jax
import jax.numpy as jnp
from jax import lax
from jax.experimental import pallas as pl
from jax.experimental.pallas import tpu as pltpu
from jax.sharding import PartitionSpec as P

f32, bf16 = jnp.float32, jnp.bfloat16
MESH = pl.DeviceIdType.MESH
CB = 256
CW = 512
OWNERS = 8


def roll(x, shift, axis):
    return pltpu.roll(x, shift % x.shape[axis], axis)


def iota(shape, dim):
    return lax.broadcasted_iota(jnp.int32, shape, dim)


def split(x):
    high = x.astype(bf16)
    return high, (x - high.astype(f32)).astype(bf16)


def dot(a, b, dims):
    return lax.dot_general(a, b, (dims, ((), ())), preferred_element_type=f32)


def dot3(a, b, dims):
    (ah, al), (bh, bl) = a, b
    return dot(ah, bh, dims) + (dot(ah, bl, dims) + dot(al, bh, dims))


NN = ((1,), (0,))
NT = ((1,), (1,))


def east(f):
    return jnp.concatenate([f[..., CB:], roll(f[..., :CB], -1, f.ndim - 1)], axis=-1)


def west(f):
    return jnp.concatenate([roll(f[..., 3 * CB :], 1, f.ndim - 1), f[..., : 3 * CB]], axis=-1)


def step(f, co):
    up, dn, ea, we = co
    ax = f.ndim - 2
    return (0.6 * f + (up * roll(f, -1, ax) + dn * roll(f, 1, ax))) + (ea * east(f) + we * west(f))


def step_t(f, co):
    up, dn, ea, we = co
    ax = f.ndim - 2
    return (0.6 * f + (roll(up * f, 1, ax) + roll(dn * f, -1, ax))) + (west(ea * f) + east(we * f))


def restrict(f):
    z = (f[:, :CB] + f[:, CB : 2 * CB]) + (f[:, 2 * CB : 3 * CB] + f[:, 3 * CB :])
    z = z + roll(z, -1, 0)
    z = (z + roll(z, -2, 0)) * (1.0 / 16.0)
    return jnp.concatenate([z[0:1], z[4:5]], axis=1)


def swap(x):
    return jnp.concatenate([x[:, CB:], x[:, :CB]], axis=1)


def col(x, d):
    if d == 0:
        return x
    return jnp.concatenate([roll(x[:, :CB], -d, 1), roll(x[:, CB:], -d, 1)], axis=1)


def stack(x):
    return jnp.concatenate([col(x, -1), x, col(x, 1)], axis=0)


def apply_k(x, ca, cb):
    reach = len(ca) // 2
    y = swap(x)
    out = None
    for d in range(-reach, reach + 1):
        term = ca[d + reach] * col(x, d) + cb[d + reach] * col(y, d)
        out = term if out is None else out + term
    return out


def apply_kt(x, ca, cb):
    reach = len(ca) // 2
    out = None
    for d in range(-reach, reach + 1):
        term = col(ca[d + reach] * x + swap(cb[d + reach] * x), -d)
        out = term if out is None else out + term
    return out


def probes(co):
    b = iota((8, 4 * CB), 1) % CB
    band = iota((8, 4 * CB), 0) // 4
    lane = iota((1, CW), 1)
    j, first = lane % CB, lane < CB

    def pair(fields):
        r0, r1 = restrict(fields[0]), restrict(fields[1])
        return jnp.where(first, r0, r1), jnp.where(first, r1, r0)

    c4 = [[jnp.zeros((1, CW), f32) for _ in range(3)] for _ in range(2)]
    c8 = [[jnp.zeros((1, CW), f32) for _ in range(5)] for _ in range(2)]

    def put(c, values, color, period):
        reach = len(c[0]) // 2
        for kind in range(2):
            for d in range(-reach, reach + 1):
                here = (j + (d + period)) % period == color
                c[kind][d + reach] = jnp.where(here, values[kind], c[kind][d + reach])

    for p in range(4):
        fields = [jnp.where((b % 4 == p) & (band == i), 1.0, 0.0).astype(f32) for i in range(2)]
        for _ in range(4):
            fields = [step(f, co) for f in fields]
        put(c4, pair(fields), p, 4)
        for p8 in (p, p + 4):
            near = (b + (9 - p8)) % 8 <= 2
            wide = [jnp.where(near, f, 0.0) for f in fields]
            for _ in range(4):
                wide = [step(f, co) for f in wide]
            put(c8, pair(wide), p8, 8)
    return c4, c8


def down(x, first):
    row = iota(x.shape, 0)
    return jnp.where(row == 0, first, roll(x, 1, 0))


def upward(x):
    row = iota(x.shape, 0)
    return jnp.where(row == x.shape[0] - 1, 0.0, roll(x, -1, 0))


def scanner(d, reverse):
    n = d.shape[0]
    row = iota(d.shape, 0)
    levels, k = [], 1
    while k < n:
        shift, ok = (-k, row < n - k) if reverse else (k, row >= k)
        levels.append((k, jnp.where(ok, d, 0.0)))
        d = d * jnp.where(ok, roll(d, shift, 0), 1.0)
        k *= 2

    def run(u):
        for k, factor in levels:
            u = u + factor * roll(u, -k if reverse else k, 0)
        return u

    return run


def sweeps(parts, r_init, a4_init, a8_init, k4, k8):
    d, src, s1, s2, q0, q1, q2 = parts
    row = iota(d.shape, 0)
    forward, backward = scanner(d, False), scanner(d, True)
    c0_next = forward(src + jnp.where(row == 0, d * r_init, 0.0))
    c0 = down(c0_next, r_init)
    rf0 = jnp.where(row == 0, a4_init, apply_k(c0, *k4)) + s1
    e1_next = forward(rf0 - c0_next)
    e1 = down(e1_next, 0.0)
    de1 = d * e1
    w = apply_k(de1, *k4) + jnp.where(row == 0, a8_init, apply_k(c0, *k8)) + s2
    rf1 = down(w, a4_init) + s1
    e2 = down(forward(rf1 - rf0 - de1), 0.0)

    lam = upward(backward(d * q0))
    r2 = q0 + lam
    r1 = upward(backward(q1 + apply_kt(lam, *k4) - d * r2))
    bb = q2 + apply_kt(lam, *k8) + apply_kt(d * (r1 - r2), *k4)
    r0 = upward(backward(upward(bb) - d * r1))
    return c0, e1, e2, r2, r1, r0


def kernel(
    count,
    initial, forcing, vel_x, vel_y, cot,
    first_hbm, bias1_hbm, middle_hbm, bias2_hbm, last_hbm, bias3_hbm,
    result,
    w1, b1, w_middle, b2, w3, b3,
    comb, gat, pack, part, full,
    s0, r0sem, s1sem, r1sem, s2sem, r2sem, s3a, s3b, r3sem, band_sem, weight_sem,
):
    me, core = lax.axis_index("tm"), lax.axis_index("space")
    other = 1 - core

    def peers(body):
        if count <= 8:
            for d in range(1, count):
                body(lax.rem(me + d, count))
        else:
            lax.fori_loop(1, count, lambda d, c: (body(lax.rem(me + d, count)), c)[1], 0)

    mine = comb.at[core]
    for k, ref in enumerate((forcing.at[0], vel_x, vel_y, initial, cot.at[0])):
        pltpu.make_async_copy(ref, mine.at[k], band_sem).start()
    loads = [
        pltpu.make_async_copy(src, dst, weight_sem.at[k])
        for k, (src, dst) in enumerate((
            (first_hbm, w1), (bias1_hbm, b1), (middle_hbm, w_middle), (bias2_hbm, b2),
            (last_hbm, w3), (bias3_hbm, b3)))]
    for load in loads:
        load.start()

    barrier = pltpu.get_barrier_semaphore()

    def greet(t, c):
        pl.semaphore_signal(barrier, inc=1, device_id={"tm": t, "space": c}, device_id_type=MESH)

    greet(me, other)
    peers(lambda t: (greet(t, core), greet(t, other)))

    def remote(src, dst, send, recv, t, c):
        return pltpu.make_async_remote_copy(
            src_ref=src, dst_ref=dst, send_sem=send, recv_sem=recv,
            device_id={"tm": t, "space": c}, device_id_type=MESH,
        )

    def drain(ref, sem):
        pltpu.make_async_copy(ref, ref, sem).wait()

    for load in loads:
        load.wait()

    mid_a = [w_middle[3 + q] for q in range(3)]
    mid_b = [w_middle[q] + w_middle[6 + q] for q in range(3)]
    mid = split(jnp.concatenate(
        [jnp.concatenate(mid_a, axis=1), jnp.concatenate(mid_b, axis=1)], axis=0))
    mid_t = split(jnp.concatenate(
        [jnp.concatenate([a, b], axis=1) for a, b in zip(mid_a, mid_b)], axis=0).T)
    fst_a = [w1[3 + q] for q in range(3)]
    fst_b = [w1[q] + w1[6 + q] for q in range(3)]
    lst_a = [w3[3 + q] for q in range(3)]
    lst_b = [w3[q] + w3[6 + q] for q in range(3)]
    lst = split(jnp.concatenate(
        [jnp.concatenate(lst_a, axis=1), jnp.concatenate(lst_b, axis=1),
         jnp.zeros((12, 192), f32)], axis=0))
    upright = jnp.concatenate(fst_a + fst_b + lst_a + lst_b + [b1[...], b2[...]], axis=0).T
    bias1, bias2 = upright[:, 30:31], upright[:, 31:32]
    b_last = b3[...]
    src_lane, dst_lane = iota((CW, CW), 0), iota((CW, CW), 1)
    order = jnp.where(src_lane == 4 * (dst_lane % 128) + dst_lane // 128, 1.0, 0.0).astype(bf16)

    pl.semaphore_wait(barrier, 2 * count - 1)
    drain(mine, band_sem)
    bands = remote(mine, mine, s0, r0sem, me, other)
    bands.start()
    bands.wait()

    rows = []
    for k in range(5):
        x = jnp.concatenate([comb[0, k], comb[1, k]], axis=0)
        rows += [x[:, :CW], x[:, CW:]]
    x = jnp.concatenate(rows, axis=0)
    high, rest = split(x)
    low = (x - high.astype(f32) - rest.astype(f32)).astype(bf16)
    y = dot(jnp.concatenate([high, rest, low], axis=0), order, NN)
    y = (y[0:80] + y[80:160]) + y[160:240]
    fields = []
    for k in range(5):
        pieces = []
        for s in range(4):
            for h in range(2):
                pieces.append(y[16 * k + 8 * h : 16 * k + 8 * h + 8, 128 * s : 128 * s + 128])
        fields.append(jnp.concatenate(pieces, axis=1))
    force, vx, vy, start, weight = fields

    inputs = [restrict(force), restrict(vx), restrict(vy)]
    pre = jnp.broadcast_to(bias1, (64, CW))
    shifted = [[col(inputs[c], q - 1) for c in range(3)] for q in range(3)]
    for q in range(3):
        for c in range(3):
            v = shifted[q][c]
            pre = pre + (upright[:, 3 * q + c : 3 * q + c + 1] * v
                         + upright[:, 9 + 3 * q + c : 10 + 3 * q + c] * swap(v))
    hidden1 = jnp.tanh(pre)
    stack1 = split(stack(hidden1))
    z = dot3(mid, stack1, NN)
    hidden2 = jnp.tanh(z[:64] + swap(z[64:]) + bias2)
    stack2f = stack(hidden2)
    z = dot3(lst, split(stack2f), NN)
    out = z[0:2] + swap(z[2:4])
    rate = 3.0 / count
    gate = 1.0 / (1.0 + jnp.exp(-(out[0:1] + b_last[0:1, 0:1])))
    decay = jnp.exp(-rate * gate)
    source = (out[1:2] + b_last[0:1, 1:2]) * (1.0 / count)

    co = (0.1 - 0.25 * vy, 0.1 + 0.25 * vy, 0.1 - 0.25 * vx, 0.1 + 0.25 * vx)
    half = 0.5 * force
    sf, av, tv = half, start, weight
    for _ in range(3):
        sf = step(sf, co) + half
    s1 = restrict(sf)
    q0 = restrict(weight)
    for _ in range(4):
        sf, tv = step(sf, co), step_t(tv, co)
    s2, q1 = restrict(sf), restrict(tv)
    for _ in range(4):
        tv = step_t(tv, co)
    q2 = restrict(tv)

    gat[me] = jnp.concatenate(
        [decay, source, s1, s2, q0, q1, q2, jnp.zeros((1, CW), f32)], axis=0)
    peers(lambda t: remote(gat.at[me], gat.at[me], s1sem, r1sem, t, core).start())

    r_init = restrict(start)
    for _ in range(4):
        av = step(av, co)
    a4_init = restrict(av)
    for _ in range(4):
        av = step(av, co)
    a8_init = restrict(av)
    k4, k8 = probes(co)

    drain(gat.at[pl.ds(0, count - 1)], r1sem)
    parts = [gat[:, k, :] for k in range(7)]
    results = sweeps(parts, r_init, a4_init, a8_init, k4, k8)
    here = iota((count, CW), 0) == me
    c0, e1, e2, r2, r1, r0 = [
        jnp.sum(jnp.where(here, v, 0.0), axis=0, keepdims=True) for v in results]
    g_decay = 16.0 * (r2 * e2 + r1 * e1 + r0 * c0)
    go = [g_decay * decay * (-rate) * gate * (1.0 - gate), r0 * (16.0 / count)]

    own = core == 0

    def kind(v):
        return jnp.where(own, v, swap(v))

    grad2 = jnp.zeros((64, CW), f32)
    for q in range(3):
        for o in range(2):
            v = col(go[o], 1 - q)
            at = 18 + 2 * q + o
            grad2 = grad2 + (
                upright[:, at : at + 1] * v + upright[:, 6 + at : 7 + at] * swap(v))
    grad2 = grad2 * (1.0 - hidden2 * hidden2)
    z = dot3(mid_t, split(jnp.concatenate([col(grad2, 1), grad2, col(grad2, -1)], axis=0)), NN)
    grad1 = (z[:64] + swap(z[64:])) * (1.0 - hidden1 * hidden1)
    gmid = dot3(split(kind(grad2)), stack1, NT)

    def lane_sum(v):
        return jnp.sum(v, axis=1, keepdims=True)

    grad1k = kind(grad1)
    gok = [kind(v) for v in go]
    columns = [lane_sum(grad1k * shifted[q][c]) for q in range(3) for c in range(3)]
    columns += [lane_sum(grad1), lane_sum(grad2)]
    columns += [
        lane_sum(gok[o] * stack2f[64 * q : 64 * q + 64]) for q in range(3) for o in range(2)]
    columns += [jnp.broadcast_to(lane_sum(v), (64, 1)) for v in go]
    lane = iota((64, 64), 1)
    tail = jnp.zeros((64, 64), f32)
    for k, v in enumerate(columns):
        tail = jnp.where(lane == k, v, tail)
    pack[...] = jnp.concatenate([gmid, tail], axis=1)

    def to_owner(t):
        return remote(pack.at[pl.ds(8 * t, 8)], part.at[me], s2sem, r2sem, t, core)

    def spread(body):
        if count == OWNERS:
            body()
        else:
            pl.when(me < OWNERS)(body)

    if count == OWNERS:
        peers(lambda t: to_owner(t).start())
        drain(part.at[pl.ds(0, count - 1)], r2sem)
    else:
        for t in range(OWNERS):
            pl.when(me != t)(lambda t=t: to_owner(t).start())
        spread(lambda: drain(part.at[pl.ds(0, count - 1)], r2sem))

    def publish():
        at = pl.multiple_of(8 * me, 8)
        part[me] = pack[pl.ds(at, 8)]
        total = part[0]
        if count <= 8:
            for t in range(1, count):
                total = total + part[t]
        else:
            total = lax.fori_loop(1, count, lambda t, acc: acc + part[t], total)
        shard = full.at[pl.ds(pl.multiple_of(64 * core + 8 * me, 8), 8)]
        shard[...] = total
        remote(shard, shard, s3b, r3sem, me, other).start()
        peers(lambda t: (remote(shard, shard, s3a, r3sem, t, core).start(),
                         remote(shard, shard, s3b, r3sem, t, other).start()))

    spread(publish)
    if count == OWNERS:
        drain(full.at[pl.ds(0, 120)], r3sem)
    else:
        pl.when(me < OWNERS)(lambda: drain(full.at[pl.ds(0, 120)], r3sem))
        pl.when(me >= OWNERS)(lambda: drain(full, r3sem))

    result[...] = full[...]

    drain(gat.at[pl.ds(0, count - 1)], s1sem)
    if count == OWNERS:
        drain(part.at[pl.ds(0, count - 1)], s2sem)
    else:
        pl.when(me < OWNERS)(lambda: drain(pack.at[pl.ds(0, 56)], s2sem))
        pl.when(me >= OWNERS)(lambda: drain(pack, s2sem))

    def sent():
        drain(part.at[pl.ds(0, count - 1)], s3a)
        drain(part, s3b)

    spread(sent)


GRADS = ((9, 3, 64), (1, 64), (9, 64, 64), (1, 64), (9, 2, 64), (1, 2))


def unpack(full, *refs):
    outs, (g_first, gb_first, g_middle, gb_middle, g_last, gb_last), sem = (
        refs[:6], refs[6:12], refs[12])
    copies = [pltpu.make_async_copy(refs[6 + k], outs[k], sem.at[k]) for k in range(6)]
    halves = [full[0:64, :], full[64:128, :]]
    for k in range(2):
        for q in range(3):
            for p in ((1,), (0, 2))[k]:
                g_middle[3 * p + q] = halves[k][:, 64 * q : 64 * q + 64]
    copies[2].start()
    for k in range(2):
        turned = halves[k][:, 128:].T
        for q in range(3):
            for p in ((1,), (0, 2))[k]:
                g_first[3 * p + q] = turned[64 + 3 * q : 67 + 3 * q, :]
                g_last[3 * p + q] = turned[75 + 2 * q : 77 + 2 * q, :]
        if k == 0:
            gb_first[...] = turned[73:74, :]
            gb_middle[...] = turned[74:75, :]
            gb_last[...] = halves[0][0:1, 209:211]
    for k in (0, 1, 3, 4, 5):
        copies[k].start()
    for copy in copies:
        copy.wait()


def per_device(count, *args):
    initial, forcing, vx, vy, cot, w1, b1, w2, b2, w3, b3 = args
    vmem, hbm = pl.BlockSpec(memory_space=pltpu.VMEM), pl.BlockSpec(memory_space=pltpu.HBM)
    dma = pltpu.SemaphoreType.DMA
    grads = [pltpu.VMEM(s, f32) for s in GRADS]
    full = pl.pallas_call(
        functools.partial(kernel, count),
        out_shape=jax.ShapeDtypeStruct((128, 256), f32),
        in_specs=[hbm] * 11,
        out_specs=vmem,
        scratch_shapes=grads + [
            pltpu.VMEM((2, 5, 4, 1024), f32),
            pltpu.VMEM((count, 8, CW), f32),
            pltpu.VMEM((64, 256), f32),
            pltpu.VMEM((count, 8, 256), f32),
            pltpu.VMEM((128, 256), f32),
        ] + [dma] * 10 + [dma((6,))],
        compiler_params=pltpu.CompilerParams(
            collective_id=0, has_side_effects=True, vmem_limit_bytes=62 * 1024 * 1024),
    )(initial, forcing, vx, vy, cot, w1.transpose(0, 2, 1), b1.reshape(1, 64), w2,
      b2.reshape(1, 64), w3, b3.reshape(1, 2))
    outs = pl.pallas_call(
        unpack,
        out_shape=[jax.ShapeDtypeStruct(s, f32) for s in GRADS],
        in_specs=[vmem],
        out_specs=[hbm] * 6,
        scratch_shapes=grads + [dma((6,))],
    )(full)
    return (outs[0].transpose(0, 2, 1), outs[1].reshape(64), outs[2], outs[3].reshape(64),
            outs[4], outs[5].reshape(2))


def solution(mesh):
    band, piece = P(("groups", "space"), None), P(("groups", "tm"), "space", None)
    return jax.shard_map(
        functools.partial(per_device, mesh.shape["tm"]),
        mesh=mesh,
        in_specs=(band, piece, band, band, piece) + (P(),) * 6,
        out_specs=(
            P("groups", None, None), P("groups"), P("groups", None, None), P("groups"),
            P("groups", None, None), P("groups"),
        ),
        check_vma=False,
    )
```

```python
import functools

import jax
import jax.numpy as jnp
from jax import lax
from jax.experimental import pallas as pl
from jax.experimental.pallas import tpu as pltpu
from jax.sharding import PartitionSpec as P

f32, bf16 = jnp.float32, jnp.bfloat16
MESH = pl.DeviceIdType.MESH
CB = 256
CW = 512
OWNERS = 8


def roll(x, shift, axis):
    return pltpu.roll(x, shift % x.shape[axis], axis)


def iota(shape, dim):
    return lax.broadcasted_iota(jnp.int32, shape, dim)


def split(x):
    high = x.astype(bf16)
    return high, (x - high.astype(f32)).astype(bf16)


def dot(a, b, dims):
    return lax.dot_general(a, b, (dims, ((), ())), preferred_element_type=f32)


def dot3(a, b, dims):
    (ah, al), (bh, bl) = a, b
    return dot(ah, bh, dims) + (dot(ah, bl, dims) + dot(al, bh, dims))


NN = ((1,), (0,))
NT = ((1,), (1,))


def east(f):
    return jnp.concatenate([f[..., CB:], roll(f[..., :CB], -1, f.ndim - 1)], axis=-1)


def west(f):
    return jnp.concatenate([roll(f[..., 3 * CB :], 1, f.ndim - 1), f[..., : 3 * CB]], axis=-1)


def step(f, co):
    up, dn, ea, we = co
    ax = f.ndim - 2
    return (0.6 * f + (up * roll(f, -1, ax) + dn * roll(f, 1, ax))) + (ea * east(f) + we * west(f))


def step_t(f, co):
    up, dn, ea, we = co
    ax = f.ndim - 2
    return (0.6 * f + (roll(up * f, 1, ax) + roll(dn * f, -1, ax))) + (west(ea * f) + east(we * f))


def restrict(f):
    z = (f[:, :CB] + f[:, CB : 2 * CB]) + (f[:, 2 * CB : 3 * CB] + f[:, 3 * CB :])
    z = z + roll(z, -1, 0)
    z = (z + roll(z, -2, 0)) * (1.0 / 16.0)
    return jnp.concatenate([z[0:1], z[4:5]], axis=1)


def swap(x):
    return jnp.concatenate([x[:, CB:], x[:, :CB]], axis=1)


def col(x, d):
    if d == 0:
        return x
    return jnp.concatenate([roll(x[:, :CB], -d, 1), roll(x[:, CB:], -d, 1)], axis=1)


def stack(x):
    return jnp.concatenate([col(x, -1), x, col(x, 1)], axis=0)


def apply_k(x, ca, cb):
    reach = len(ca) // 2
    y = swap(x)
    out = None
    for d in range(-reach, reach + 1):
        term = ca[d + reach] * col(x, d) + cb[d + reach] * col(y, d)
        out = term if out is None else out + term
    return out


def apply_kt(x, ca, cb):
    reach = len(ca) // 2
    out = None
    for d in range(-reach, reach + 1):
        term = col(ca[d + reach] * x + swap(cb[d + reach] * x), -d)
        out = term if out is None else out + term
    return out


def probes(co):
    b = iota((8, 4 * CB), 1) % CB
    band = iota((8, 4 * CB), 0) // 4
    lane = iota((1, CW), 1)
    j, first = lane % CB, lane < CB

    def pair(fields):
        r0, r1 = restrict(fields[0]), restrict(fields[1])
        return jnp.where(first, r0, r1), jnp.where(first, r1, r0)

    c4 = [[jnp.zeros((1, CW), f32) for _ in range(3)] for _ in range(2)]
    c8 = [[jnp.zeros((1, CW), f32) for _ in range(5)] for _ in range(2)]

    def put(c, values, color, period):
        reach = len(c[0]) // 2
        for kind in range(2):
            for d in range(-reach, reach + 1):
                here = (j + (d + period)) % period == color
                c[kind][d + reach] = jnp.where(here, values[kind], c[kind][d + reach])

    for p in range(4):
        fields = [jnp.where((b % 4 == p) & (band == i), 1.0, 0.0).astype(f32) for i in range(2)]
        for _ in range(4):
            fields = [step(f, co) for f in fields]
        put(c4, pair(fields), p, 4)
        for p8 in (p, p + 4):
            near = (b + (9 - p8)) % 8 <= 2
            wide = [jnp.where(near, f, 0.0) for f in fields]
            for _ in range(4):
                wide = [step(f, co) for f in wide]
            put(c8, pair(wide), p8, 8)
    return c4, c8


def down(x, first):
    row = iota(x.shape, 0)
    return jnp.where(row == 0, first, roll(x, 1, 0))


def upward(x):
    row = iota(x.shape, 0)
    return jnp.where(row == x.shape[0] - 1, 0.0, roll(x, -1, 0))


def scanner(d, reverse):
    n = d.shape[0]
    row = iota(d.shape, 0)
    levels, k = [], 1
    while k < n:
        shift, ok = (-k, row < n - k) if reverse else (k, row >= k)
        levels.append((k, jnp.where(ok, d, 0.0)))
        d = d * jnp.where(ok, roll(d, shift, 0), 1.0)
        k *= 2

    def run(u):
        for k, factor in levels:
            u = u + factor * roll(u, -k if reverse else k, 0)
        return u

    return run


def sweeps(parts, r_init, a4_init, a8_init, k4, k8):
    d, src, s1, s2, q0, q1, q2 = parts
    row = iota(d.shape, 0)
    forward, backward = scanner(d, False), scanner(d, True)
    c0_next = forward(src + jnp.where(row == 0, d * r_init, 0.0))
    c0 = down(c0_next, r_init)
    rf0 = jnp.where(row == 0, a4_init, apply_k(c0, *k4)) + s1
    e1_next = forward(rf0 - c0_next)
    e1 = down(e1_next, 0.0)
    de1 = d * e1
    w = apply_k(de1, *k4) + jnp.where(row == 0, a8_init, apply_k(c0, *k8)) + s2
    rf1 = down(w, a4_init) + s1
    e2 = down(forward(rf1 - rf0 - de1), 0.0)

    lam = upward(backward(d * q0))
    r2 = q0 + lam
    r1 = upward(backward(q1 + apply_kt(lam, *k4) - d * r2))
    bb = q2 + apply_kt(lam, *k8) + apply_kt(d * (r1 - r2), *k4)
    r0 = upward(backward(upward(bb) - d * r1))
    return c0, e1, e2, r2, r1, r0


def kernel(
    count,
    initial, forcing, vel_x, vel_y, cot,
    first_hbm, bias1_hbm, middle_hbm, bias2_hbm, last_hbm, bias3_hbm,
    result,
    w1, b1, w_middle, b2, w3, b3,
    raw, comb, gat, pack, part, full,
    s0, r0sem, s1sem, r1sem, s2sem, r2sem, s3a, s3b, r3sem, band_sem, weight_sem,
):
    me, core = lax.axis_index("tm"), lax.axis_index("space")
    other = 1 - core

    def peers(body):
        if count <= 8:
            for d in range(1, count):
                body(lax.rem(me + d, count))
        else:
            lax.fori_loop(1, count, lambda d, c: (body(lax.rem(me + d, count)), c)[1], 0)

    mine = comb.at[core]
    for k, ref in enumerate((forcing.at[0], vel_x, vel_y, initial, cot.at[0])):
        pltpu.make_async_copy(ref, raw.at[k], band_sem).start()
    loads = [
        pltpu.make_async_copy(src, dst, weight_sem.at[k])
        for k, (src, dst) in enumerate((
            (first_hbm, w1), (bias1_hbm, b1), (middle_hbm, w_middle), (bias2_hbm, b2),
            (last_hbm, w3), (bias3_hbm, b3)))]
    for load in loads:
        load.start()

    barrier = pltpu.get_barrier_semaphore()

    def greet(t, c):
        pl.semaphore_signal(barrier, inc=1, device_id={"tm": t, "space": c}, device_id_type=MESH)

    greet(me, other)
    peers(lambda t: (greet(t, core), greet(t, other)))

    def remote(src, dst, send, recv, t, c):
        return pltpu.make_async_remote_copy(
            src_ref=src, dst_ref=dst, send_sem=send, recv_sem=recv,
            device_id={"tm": t, "space": c}, device_id_type=MESH,
        )

    def drain(ref, sem):
        pltpu.make_async_copy(ref, ref, sem).wait()

    src_lane, dst_lane = iota((CW, CW), 0), iota((CW, CW), 1)
    order = jnp.where(src_lane == 4 * (dst_lane % 128) + dst_lane // 128, 1.0, 0.0).astype(bf16)
    drain(raw, band_sem)
    x = jnp.concatenate([raw[k] for k in range(5)] + [jnp.zeros((4, 1024), f32)], axis=0)
    x = jnp.concatenate([x[:, :CW], x[:, CW:]], axis=0)
    high, rest = split(x)
    low = (x - high.astype(f32) - rest.astype(f32)).astype(bf16)
    y = dot(jnp.concatenate([high, rest, low], axis=0), order, NN)
    y = (y[0:48] + y[48:96]) + y[96:144]
    for k in range(5):
        for s in range(4):
            for h in range(2):
                at = CB * s + 128 * h
                mine[k, :, at : at + 128] = y[
                    24 * h + 4 * k : 24 * h + 4 * k + 4, 128 * s : 128 * s + 128]

    pl.semaphore_wait(barrier, 2 * count - 1)
    bands = remote(mine, mine, s0, r0sem, me, other)
    bands.start()

    for load in loads:
        load.wait()

    mid_a = [w_middle[3 + q] for q in range(3)]
    mid_b = [w_middle[q] + w_middle[6 + q] for q in range(3)]
    mid = split(jnp.concatenate(
        [jnp.concatenate(mid_a, axis=1), jnp.concatenate(mid_b, axis=1)], axis=0))
    mid_t = split(jnp.concatenate(
        [jnp.concatenate([a, b], axis=1) for a, b in zip(mid_a, mid_b)], axis=0).T)
    fst_a = [w1[3 + q] for q in range(3)]
    fst_b = [w1[q] + w1[6 + q] for q in range(3)]
    lst_a = [w3[3 + q] for q in range(3)]
    lst_b = [w3[q] + w3[6 + q] for q in range(3)]
    lst = split(jnp.concatenate(
        [jnp.concatenate(lst_a, axis=1), jnp.concatenate(lst_b, axis=1),
         jnp.zeros((12, 192), f32)], axis=0))
    upright = jnp.concatenate(fst_a + fst_b + lst_a + lst_b + [b1[...], b2[...]], axis=0).T
    bias1, bias2 = upright[:, 30:31], upright[:, 31:32]
    b_last = b3[...]

    bands.wait()
    force, vx, vy, start, weight = [
        jnp.concatenate([comb[0, k], comb[1, k]], axis=0) for k in range(5)]

    inputs = [restrict(force), restrict(vx), restrict(vy)]
    pre = jnp.broadcast_to(bias1, (64, CW))
    shifted = [[col(inputs[c], q - 1) for c in range(3)] for q in range(3)]
    for q in range(3):
        for c in range(3):
            v = shifted[q][c]
            pre = pre + (upright[:, 3 * q + c : 3 * q + c + 1] * v
                         + upright[:, 9 + 3 * q + c : 10 + 3 * q + c] * swap(v))
    hidden1 = jnp.tanh(pre)
    stack1 = split(stack(hidden1))
    z = dot3(mid, stack1, NN)
    hidden2 = jnp.tanh(z[:64] + swap(z[64:]) + bias2)
    stack2f = stack(hidden2)
    z = dot3(lst, split(stack2f), NN)
    out = z[0:2] + swap(z[2:4])
    rate = 3.0 / count
    gate = 1.0 / (1.0 + jnp.exp(-(out[0:1] + b_last[0:1, 0:1])))
    decay = jnp.exp(-rate * gate)
    source = (out[1:2] + b_last[0:1, 1:2]) * (1.0 / count)

    co = (0.1 - 0.25 * vy, 0.1 + 0.25 * vy, 0.1 - 0.25 * vx, 0.1 + 0.25 * vx)
    half = 0.5 * force
    sf, av, tv = half, start, weight
    for _ in range(3):
        sf = step(sf, co) + half
    s1 = restrict(sf)
    q0 = restrict(weight)
    for _ in range(4):
        sf, tv = step(sf, co), step_t(tv, co)
    s2, q1 = restrict(sf), restrict(tv)
    for _ in range(4):
        tv = step_t(tv, co)
    q2 = restrict(tv)

    gat[me] = jnp.concatenate(
        [decay, source, s1, s2, q0, q1, q2, jnp.zeros((1, CW), f32)], axis=0)
    peers(lambda t: remote(gat.at[me], gat.at[me], s1sem, r1sem, t, core).start())

    r_init = restrict(start)
    for _ in range(4):
        av = step(av, co)
    a4_init = restrict(av)
    for _ in range(4):
        av = step(av, co)
    a8_init = restrict(av)
    k4, k8 = probes(co)

    drain(gat.at[pl.ds(0, count - 1)], r1sem)
    parts = [gat[:, k, :] for k in range(7)]
    results = sweeps(parts, r_init, a4_init, a8_init, k4, k8)
    here = iota((count, CW), 0) == me
    c0, e1, e2, r2, r1, r0 = [
        jnp.sum(jnp.where(here, v, 0.0), axis=0, keepdims=True) for v in results]
    g_decay = 16.0 * (r2 * e2 + r1 * e1 + r0 * c0)
    go = [g_decay * decay * (-rate) * gate * (1.0 - gate), r0 * (16.0 / count)]

    own = core == 0

    def kind(v):
        return jnp.where(own, v, swap(v))

    grad2 = jnp.zeros((64, CW), f32)
    for q in range(3):
        for o in range(2):
            v = col(go[o], 1 - q)
            at = 18 + 2 * q + o
            grad2 = grad2 + (
                upright[:, at : at + 1] * v + upright[:, 6 + at : 7 + at] * swap(v))
    grad2 = grad2 * (1.0 - hidden2 * hidden2)
    z = dot3(mid_t, split(jnp.concatenate([col(grad2, 1), grad2, col(grad2, -1)], axis=0)), NN)
    grad1 = (z[:64] + swap(z[64:])) * (1.0 - hidden1 * hidden1)
    gmid = dot3(split(kind(grad2)), stack1, NT)

    def lane_sum(v):
        return jnp.sum(v, axis=1, keepdims=True)

    grad1k = kind(grad1)
    gok = [kind(v) for v in go]
    columns = [lane_sum(grad1k * shifted[q][c]) for q in range(3) for c in range(3)]
    columns += [lane_sum(grad1), lane_sum(grad2)]
    columns += [
        lane_sum(gok[o] * stack2f[64 * q : 64 * q + 64]) for q in range(3) for o in range(2)]
    columns += [jnp.broadcast_to(lane_sum(v), (64, 1)) for v in go]
    lane = iota((64, 64), 1)
    tail = jnp.zeros((64, 64), f32)
    for k, v in enumerate(columns):
        tail = jnp.where(lane == k, v, tail)
    pack[...] = jnp.concatenate([gmid, tail], axis=1)

    def to_owner(t):
        return remote(pack.at[pl.ds(8 * t, 8)], part.at[me], s2sem, r2sem, t, core)

    def spread(body):
        if count == OWNERS:
            body()
        else:
            pl.when(me < OWNERS)(body)

    if count == OWNERS:
        peers(lambda t: to_owner(t).start())
        drain(part.at[pl.ds(0, count - 1)], r2sem)
    else:
        for t in range(OWNERS):
            pl.when(me != t)(lambda t=t: to_owner(t).start())
        spread(lambda: drain(part.at[pl.ds(0, count - 1)], r2sem))

    def publish():
        at = pl.multiple_of(8 * me, 8)
        part[me] = pack[pl.ds(at, 8)]
        total = part[0]
        if count <= 8:
            for t in range(1, count):
                total = total + part[t]
        else:
            total = lax.fori_loop(1, count, lambda t, acc: acc + part[t], total)
        shard = full.at[pl.ds(pl.multiple_of(64 * core + 8 * me, 8), 8)]
        shard[...] = total
        remote(shard, shard, s3b, r3sem, me, other).start()
        peers(lambda t: (remote(shard, shard, s3a, r3sem, t, core).start(),
                         remote(shard, shard, s3b, r3sem, t, other).start()))

    spread(publish)
    if count == OWNERS:
        drain(full.at[pl.ds(0, 120)], r3sem)
    else:
        pl.when(me < OWNERS)(lambda: drain(full.at[pl.ds(0, 120)], r3sem))
        pl.when(me >= OWNERS)(lambda: drain(full, r3sem))

    result[...] = full[...]

    drain(gat.at[pl.ds(0, count - 1)], s1sem)
    if count == OWNERS:
        drain(part.at[pl.ds(0, count - 1)], s2sem)
    else:
        pl.when(me < OWNERS)(lambda: drain(pack.at[pl.ds(0, 56)], s2sem))
        pl.when(me >= OWNERS)(lambda: drain(pack, s2sem))

    def sent():
        drain(part.at[pl.ds(0, count - 1)], s3a)
        drain(part, s3b)

    spread(sent)


GRADS = ((9, 3, 64), (1, 64), (9, 64, 64), (1, 64), (9, 2, 64), (1, 2))


def unpack(full, *refs):
    outs, (g_first, gb_first, g_middle, gb_middle, g_last, gb_last), sem = (
        refs[:6], refs[6:12], refs[12])
    copies = [pltpu.make_async_copy(refs[6 + k], outs[k], sem.at[k]) for k in range(6)]
    halves = [full[0:64, :], full[64:128, :]]
    for k in range(2):
        for q in range(3):
            for p in ((1,), (0, 2))[k]:
                g_middle[3 * p + q] = halves[k][:, 64 * q : 64 * q + 64]
    copies[2].start()
    for k in range(2):
        turned = halves[k][:, 128:].T
        for q in range(3):
            for p in ((1,), (0, 2))[k]:
                g_first[3 * p + q] = turned[64 + 3 * q : 67 + 3 * q, :]
                g_last[3 * p + q] = turned[75 + 2 * q : 77 + 2 * q, :]
        if k == 0:
            gb_first[...] = turned[73:74, :]
            gb_middle[...] = turned[74:75, :]
            gb_last[...] = halves[0][0:1, 209:211]
    for k in (0, 1, 3, 4, 5):
        copies[k].start()
    for copy in copies:
        copy.wait()


def per_device(count, *args):
    initial, forcing, vx, vy, cot, w1, b1, w2, b2, w3, b3 = args
    vmem, hbm = pl.BlockSpec(memory_space=pltpu.VMEM), pl.BlockSpec(memory_space=pltpu.HBM)
    dma = pltpu.SemaphoreType.DMA
    grads = [pltpu.VMEM(s, f32) for s in GRADS]
    full = pl.pallas_call(
        functools.partial(kernel, count),
        out_shape=jax.ShapeDtypeStruct((128, 256), f32),
        in_specs=[hbm] * 11,
        out_specs=vmem,
        scratch_shapes=grads + [
            pltpu.VMEM((5, 4, 1024), f32),
            pltpu.VMEM((2, 5, 4, 1024), f32),
            pltpu.VMEM((count, 8, CW), f32),
            pltpu.VMEM((64, 256), f32),
            pltpu.VMEM((count, 8, 256), f32),
            pltpu.VMEM((128, 256), f32),
        ] + [dma] * 10 + [dma((6,))],
        compiler_params=pltpu.CompilerParams(
            collective_id=0, has_side_effects=True, vmem_limit_bytes=62 * 1024 * 1024),
    )(initial, forcing, vx, vy, cot, w1.transpose(0, 2, 1), b1.reshape(1, 64), w2,
      b2.reshape(1, 64), w3, b3.reshape(1, 2))
    outs = pl.pallas_call(
        unpack,
        out_shape=[jax.ShapeDtypeStruct(s, f32) for s in GRADS],
        in_specs=[vmem],
        out_specs=[hbm] * 6,
        scratch_shapes=grads + [dma((6,))],
    )(full)
    return (outs[0].transpose(0, 2, 1), outs[1].reshape(64), outs[2], outs[3].reshape(64),
            outs[4], outs[5].reshape(2))


def solution(mesh):
    band, piece = P(("groups", "space"), None), P(("groups", "tm"), "space", None)
    return jax.shard_map(
        functools.partial(per_device, mesh.shape["tm"]),
        mesh=mesh,
        in_specs=(band, piece, band, band, piece) + (P(),) * 6,
        out_specs=(
            P("groups", None, None), P("groups"), P("groups", None, None), P("groups"),
            P("groups", None, None), P("groups"),
        ),
        check_vma=False,
    )
```

```python
import functools

import jax
import jax.numpy as jnp
from jax import lax
from jax.experimental import pallas as pl
from jax.experimental.pallas import tpu as pltpu
from jax.sharding import PartitionSpec as P

f32, bf16 = jnp.float32, jnp.bfloat16
MESH = pl.DeviceIdType.MESH
CB = 256
CW = 512
OWNERS = 8


def roll(x, shift, axis):
    return pltpu.roll(x, shift % x.shape[axis], axis)


def iota(shape, dim):
    return lax.broadcasted_iota(jnp.int32, shape, dim)


def split(x):
    high = x.astype(bf16)
    return high, (x - high.astype(f32)).astype(bf16)


def dot(a, b, dims):
    return lax.dot_general(a, b, (dims, ((), ())), preferred_element_type=f32)


def dot3(a, b, dims):
    (ah, al), (bh, bl) = a, b
    return dot(ah, bh, dims) + (dot(ah, bl, dims) + dot(al, bh, dims))


NN = ((1,), (0,))
NT = ((1,), (1,))


def east(f):
    return jnp.concatenate([f[..., CB:], roll(f[..., :CB], -1, f.ndim - 1)], axis=-1)


def west(f):
    return jnp.concatenate([roll(f[..., 3 * CB :], 1, f.ndim - 1), f[..., : 3 * CB]], axis=-1)


def step(f, co):
    up, dn, ea, we = co
    ax = f.ndim - 2
    return (0.6 * f + (up * roll(f, -1, ax) + dn * roll(f, 1, ax))) + (ea * east(f) + we * west(f))


def step_t(f, co):
    up, dn, ea, we = co
    ax = f.ndim - 2
    return (0.6 * f + (roll(up * f, 1, ax) + roll(dn * f, -1, ax))) + (west(ea * f) + east(we * f))


def restrict(f):
    z = (f[:, :CB] + f[:, CB : 2 * CB]) + (f[:, 2 * CB : 3 * CB] + f[:, 3 * CB :])
    z = z + roll(z, -1, 0)
    z = (z + roll(z, -2, 0)) * (1.0 / 16.0)
    return jnp.concatenate([z[0:1], z[4:5]], axis=1)


def swap(x):
    return jnp.concatenate([x[:, CB:], x[:, :CB]], axis=1)


def col(x, d):
    if d == 0:
        return x
    return jnp.concatenate([roll(x[:, :CB], -d, 1), roll(x[:, CB:], -d, 1)], axis=1)


def stack(x):
    return jnp.concatenate([col(x, -1), x, col(x, 1)], axis=0)


def apply_k(x, ca, cb):
    reach = len(ca) // 2
    y = swap(x)
    out = None
    for d in range(-reach, reach + 1):
        term = ca[d + reach] * col(x, d) + cb[d + reach] * col(y, d)
        out = term if out is None else out + term
    return out


def apply_kt(x, ca, cb):
    reach = len(ca) // 2
    out = None
    for d in range(-reach, reach + 1):
        term = col(ca[d + reach] * x + swap(cb[d + reach] * x), -d)
        out = term if out is None else out + term
    return out


def probes(co):
    b = iota((8, 4 * CB), 1) % CB
    band = iota((8, 4 * CB), 0) // 4
    lane = iota((1, CW), 1)
    j, first = lane % CB, lane < CB

    def pair(fields):
        r0, r1 = restrict(fields[0]), restrict(fields[1])
        return jnp.where(first, r0, r1), jnp.where(first, r1, r0)

    c4 = [[jnp.zeros((1, CW), f32) for _ in range(3)] for _ in range(2)]
    c8 = [[jnp.zeros((1, CW), f32) for _ in range(5)] for _ in range(2)]

    def put(c, values, color, period):
        reach = len(c[0]) // 2
        for kind in range(2):
            for d in range(-reach, reach + 1):
                here = (j + (d + period)) % period == color
                c[kind][d + reach] = jnp.where(here, values[kind], c[kind][d + reach])

    for p in range(4):
        fields = [jnp.where((b % 4 == p) & (band == i), 1.0, 0.0).astype(f32) for i in range(2)]
        for _ in range(4):
            fields = [step(f, co) for f in fields]
        put(c4, pair(fields), p, 4)
        for p8 in (p, p + 4):
            near = (b + (9 - p8)) % 8 <= 2
            wide = [jnp.where(near, f, 0.0) for f in fields]
            for _ in range(4):
                wide = [step(f, co) for f in wide]
            put(c8, pair(wide), p8, 8)
    return c4, c8


def down(x, first):
    row = iota(x.shape, 0)
    return jnp.where(row == 0, first, roll(x, 1, 0))


def upward(x):
    row = iota(x.shape, 0)
    return jnp.where(row == x.shape[0] - 1, 0.0, roll(x, -1, 0))


def scanner(d, reverse):
    n = d.shape[0]
    row = iota(d.shape, 0)
    levels, k = [], 1
    while k < n:
        shift, ok = (-k, row < n - k) if reverse else (k, row >= k)
        levels.append((k, jnp.where(ok, d, 0.0)))
        d = d * jnp.where(ok, roll(d, shift, 0), 1.0)
        k *= 2

    def run(u):
        for k, factor in levels:
            u = u + factor * roll(u, -k if reverse else k, 0)
        return u

    return run


def sweeps(parts, r_init, a4_init, a8_init, k4, k8):
    d, src, s1, s2, q0, q1, q2 = parts
    row = iota(d.shape, 0)
    forward, backward = scanner(d, False), scanner(d, True)
    c0_next = forward(src + jnp.where(row == 0, d * r_init, 0.0))
    c0 = down(c0_next, r_init)
    rf0 = jnp.where(row == 0, a4_init, apply_k(c0, *k4)) + s1
    e1_next = forward(rf0 - c0_next)
    e1 = down(e1_next, 0.0)
    de1 = d * e1
    w = apply_k(de1, *k4) + jnp.where(row == 0, a8_init, apply_k(c0, *k8)) + s2
    rf1 = down(w, a4_init) + s1
    e2 = down(forward(rf1 - rf0 - de1), 0.0)

    lam = upward(backward(d * q0))
    r2 = q0 + lam
    r1 = upward(backward(q1 + apply_kt(lam, *k4) - d * r2))
    bb = q2 + apply_kt(lam, *k8) + apply_kt(d * (r1 - r2), *k4)
    r0 = upward(backward(upward(bb) - d * r1))
    return c0, e1, e2, r2, r1, r0


def kernel(
    count,
    initial, forcing, vel_x, vel_y, cot,
    first_hbm, bias1_hbm, middle_hbm, bias2_hbm, last_hbm, bias3_hbm,
    result,
    w1, b1, w_middle, b2, w3, b3,
    raw, comb, gat, pack, part, full,
    s0, r0sem, s1sem, r1sem, s2sem, r2sem, s3a, s3b, r3sem, band_sem, weight_sem,
):
    me, core = lax.axis_index("tm"), lax.axis_index("space")
    other = 1 - core

    def peers(body):
        if count <= 8:
            for d in range(1, count):
                body(lax.rem(me + d, count))
        else:
            lax.fori_loop(1, count, lambda d, c: (body(lax.rem(me + d, count)), c)[1], 0)

    mine = comb.at[core]
    for k, ref in enumerate((forcing.at[0], vel_x, vel_y, initial, cot.at[0])):
        pltpu.make_async_copy(ref, raw.at[k], band_sem).start()
    loads = [
        pltpu.make_async_copy(src, dst, weight_sem.at[k])
        for k, (src, dst) in enumerate((
            (first_hbm, w1), (bias1_hbm, b1), (middle_hbm, w_middle), (bias2_hbm, b2),
            (last_hbm, w3), (bias3_hbm, b3)))]
    for load in loads:
        load.start()

    barrier = pltpu.get_barrier_semaphore()

    def greet(t, c):
        pl.semaphore_signal(barrier, inc=1, device_id={"tm": t, "space": c}, device_id_type=MESH)

    greet(me, other)
    peers(lambda t: (greet(t, core), greet(t, other)))

    def remote(src, dst, send, recv, t, c):
        return pltpu.make_async_remote_copy(
            src_ref=src, dst_ref=dst, send_sem=send, recv_sem=recv,
            device_id={"tm": t, "space": c}, device_id_type=MESH,
        )

    def drain(ref, sem):
        pltpu.make_async_copy(ref, ref, sem).wait()

    src_lane, dst_lane = iota((CW, CW), 0), iota((CW, CW), 1)
    order = jnp.where(src_lane == 4 * (dst_lane % 128) + dst_lane // 128, 1.0, 0.0).astype(bf16)
    drain(raw, band_sem)
    x = jnp.concatenate([raw[k] for k in range(5)] + [jnp.zeros((4, 1024), f32)], axis=0)
    x = jnp.concatenate([x[:, :CW], x[:, CW:]], axis=0)
    high, rest = split(x)
    low = (x - high.astype(f32) - rest.astype(f32)).astype(bf16)
    y = dot(jnp.concatenate([high, rest, low], axis=0), order, NN)
    y = (y[0:48] + y[48:96]) + y[96:144]
    for k in range(5):
        for s in range(4):
            for h in range(2):
                at = CB * s + 128 * h
                mine[k, :, at : at + 128] = y[
                    24 * h + 4 * k : 24 * h + 4 * k + 4, 128 * s : 128 * s + 128]

    pl.semaphore_wait(barrier, 2 * count - 1)
    bands = remote(mine, mine, s0, r0sem, me, other)
    bands.start()

    for load in loads:
        load.wait()

    mid_a = [w_middle[3 + q] for q in range(3)]
    mid_b = [w_middle[q] + w_middle[6 + q] for q in range(3)]
    mid = split(jnp.concatenate(
        [jnp.concatenate(mid_a, axis=1), jnp.concatenate(mid_b, axis=1)], axis=0))
    mid_t = split(jnp.concatenate(
        [jnp.concatenate([a, b], axis=1) for a, b in zip(mid_a, mid_b)], axis=0).T)
    fst_a = [w1[3 + q] for q in range(3)]
    fst_b = [w1[q] + w1[6 + q] for q in range(3)]
    lst_a = [w3[3 + q] for q in range(3)]
    lst_b = [w3[q] + w3[6 + q] for q in range(3)]
    lst = split(jnp.concatenate(
        [jnp.concatenate(lst_a, axis=1), jnp.concatenate(lst_b, axis=1),
         jnp.zeros((12, 192), f32)], axis=0))
    upright = jnp.concatenate(fst_a + fst_b + lst_a + lst_b + [b1[...], b2[...]], axis=0).T
    bias1, bias2 = upright[:, 30:31], upright[:, 31:32]
    b_last = b3[...]

    bands.wait()
    force, vx, vy, start, weight = [
        jnp.concatenate([comb[0, k], comb[1, k]], axis=0) for k in range(5)]

    inputs = [restrict(force), restrict(vx), restrict(vy)]
    pre = jnp.broadcast_to(bias1, (64, CW))
    shifted = [[col(inputs[c], q - 1) for c in range(3)] for q in range(3)]
    for q in range(3):
        for c in range(3):
            v = shifted[q][c]
            pre = pre + (upright[:, 3 * q + c : 3 * q + c + 1] * v
                         + upright[:, 9 + 3 * q + c : 10 + 3 * q + c] * swap(v))
    hidden1 = jnp.tanh(pre)
    stack1 = split(stack(hidden1))
    z = dot3(mid, stack1, NN)
    hidden2 = jnp.tanh(z[:64] + swap(z[64:]) + bias2)
    stack2f = stack(hidden2)
    z = dot3(lst, split(stack2f), NN)
    out = z[0:2] + swap(z[2:4])
    rate = 3.0 / count
    gate = 1.0 / (1.0 + jnp.exp(-(out[0:1] + b_last[0:1, 0:1])))
    decay = jnp.exp(-rate * gate)
    source = (out[1:2] + b_last[0:1, 1:2]) * (1.0 / count)

    co = (0.1 - 0.25 * vy, 0.1 + 0.25 * vy, 0.1 - 0.25 * vx, 0.1 + 0.25 * vx)
    half = 0.5 * force
    sf, av, tv = half, start, weight
    for _ in range(3):
        sf = step(sf, co) + half
    s1 = restrict(sf)
    q0 = restrict(weight)
    for _ in range(4):
        sf, tv = step(sf, co), step_t(tv, co)
    s2, q1 = restrict(sf), restrict(tv)
    for _ in range(4):
        tv = step_t(tv, co)
    q2 = restrict(tv)

    gat[me] = jnp.concatenate(
        [decay, source, s1, s2, q0, q1, q2, jnp.zeros((1, CW), f32)], axis=0)
    peers(lambda t: remote(gat.at[me], gat.at[me], s1sem, r1sem, t, core).start())

    r_init = restrict(start)
    for _ in range(4):
        av = step(av, co)
    a4_init = restrict(av)
    for _ in range(4):
        av = step(av, co)
    a8_init = restrict(av)
    k4, k8 = probes(co)

    drain(gat.at[pl.ds(0, count - 1)], r1sem)
    parts = [gat[:, k, :] for k in range(7)]
    results = sweeps(parts, r_init, a4_init, a8_init, k4, k8)
    here = iota((count, CW), 0) == me
    c0, e1, e2, r2, r1, r0 = [
        jnp.sum(jnp.where(here, v, 0.0), axis=0, keepdims=True) for v in results]
    g_decay = 16.0 * (r2 * e2 + r1 * e1 + r0 * c0)
    go = [g_decay * decay * (-rate) * gate * (1.0 - gate), r0 * (16.0 / count)]

    own = core == 0

    def kind(v):
        return jnp.where(own, v, swap(v))

    grad2 = jnp.zeros((64, CW), f32)
    for q in range(3):
        for o in range(2):
            v = col(go[o], 1 - q)
            at = 18 + 2 * q + o
            grad2 = grad2 + (
                upright[:, at : at + 1] * v + upright[:, 6 + at : 7 + at] * swap(v))
    grad2 = grad2 * (1.0 - hidden2 * hidden2)
    def to_owner(t, h):
        return remote(
            pack.at[h, pl.ds(8 * t, 8)], part.at[h, me], s2sem.at[h], r2sem.at[h], t, core)

    def contribute(h):
        if count == OWNERS:
            peers(lambda t: to_owner(t, h).start())
        else:
            for t in range(OWNERS):
                pl.when(me != t)(lambda t=t: to_owner(t, h).start())

    def spread(body):
        if count == OWNERS:
            body()
        else:
            pl.when(me < OWNERS)(body)

    def publish(h):
        drain(part.at[h, pl.ds(0, count - 1)], r2sem.at[h])
        part[h, me] = pack[h, pl.ds(pl.multiple_of(8 * me, 8), 8)]
        total = part[h, 0]
        if count <= 8:
            for t in range(1, count):
                total = total + part[h, t]
        else:
            total = lax.fori_loop(1, count, lambda t, acc: acc + part[h, t], total)
        shard = full.at[h, pl.ds(pl.multiple_of(64 * core + 8 * me, 8), 8)]
        shard[...] = total
        peers(lambda t: (remote(shard, shard, s3a.at[h], r3sem.at[h], t, core).start(),
                         remote(shard, shard, s3b.at[h], r3sem.at[h], t, other).start()))
        remote(shard, shard, s3b.at[h], r3sem.at[h], me, other).start()

    gmid = dot3(split(kind(grad2)), stack1, NT)
    pack[0] = gmid[:, :128]
    contribute(0)

    z = dot3(mid_t, split(jnp.concatenate([col(grad2, 1), grad2, col(grad2, -1)], axis=0)), NN)
    grad1 = (z[:64] + swap(z[64:])) * (1.0 - hidden1 * hidden1)

    def lane_sum(v):
        return jnp.sum(v, axis=1, keepdims=True)

    grad1k = kind(grad1)
    gok = [kind(v) for v in go]
    columns = [lane_sum(grad1k * shifted[q][c]) for q in range(3) for c in range(3)]
    columns += [lane_sum(grad1), lane_sum(grad2)]
    columns += [
        lane_sum(gok[o] * stack2f[64 * q : 64 * q + 64]) for q in range(3) for o in range(2)]
    columns += [jnp.broadcast_to(lane_sum(v), (64, 1)) for v in go]
    lane = iota((64, 64), 1)
    tail = jnp.zeros((64, 64), f32)
    for k, v in enumerate(columns):
        tail = jnp.where(lane == k, v, tail)
    pack[1] = jnp.concatenate([gmid[:, 128:], tail], axis=1)
    contribute(1)
    for h in range(2):
        spread(lambda: publish(h))
    for h in range(2):
        if count == OWNERS:
            drain(full.at[h, pl.ds(0, 120)], r3sem.at[h])
        else:
            pl.when(me < OWNERS)(lambda: drain(full.at[h, pl.ds(0, 120)], r3sem.at[h]))
            pl.when(me >= OWNERS)(lambda: drain(full.at[h], r3sem.at[h]))

    result[...] = jnp.concatenate([full[0], full[1]], axis=1)

    drain(gat.at[pl.ds(0, count - 1)], s1sem)
    for h in range(2):
        if count == OWNERS:
            drain(part.at[h, pl.ds(0, count - 1)], s2sem.at[h])
        else:
            pl.when(me < OWNERS)(lambda: drain(pack.at[h, pl.ds(0, 56)], s2sem.at[h]))
            pl.when(me >= OWNERS)(lambda: drain(pack.at[h], s2sem.at[h]))

    def sent(h):
        drain(part.at[h, pl.ds(0, count - 1)], s3a.at[h])
        drain(part.at[h], s3b.at[h])

    for h in range(2):
        spread(lambda: sent(h))


GRADS = ((9, 3, 64), (1, 64), (9, 64, 64), (1, 64), (9, 2, 64), (1, 2))


def unpack(full, *refs):
    outs, (g_first, gb_first, g_middle, gb_middle, g_last, gb_last), sem = (
        refs[:6], refs[6:12], refs[12])
    copies = [pltpu.make_async_copy(refs[6 + k], outs[k], sem.at[k]) for k in range(6)]
    halves = [full[0:64, :], full[64:128, :]]
    for k in range(2):
        for q in range(3):
            for p in ((1,), (0, 2))[k]:
                g_middle[3 * p + q] = halves[k][:, 64 * q : 64 * q + 64]
    copies[2].start()
    for k in range(2):
        turned = halves[k][:, 128:].T
        for q in range(3):
            for p in ((1,), (0, 2))[k]:
                g_first[3 * p + q] = turned[64 + 3 * q : 67 + 3 * q, :]
                g_last[3 * p + q] = turned[75 + 2 * q : 77 + 2 * q, :]
        if k == 0:
            gb_first[...] = turned[73:74, :]
            gb_middle[...] = turned[74:75, :]
            gb_last[...] = halves[0][0:1, 209:211]
    for k in (0, 1, 3, 4, 5):
        copies[k].start()
    for copy in copies:
        copy.wait()


def per_device(count, *args):
    initial, forcing, vx, vy, cot, w1, b1, w2, b2, w3, b3 = args
    vmem, hbm = pl.BlockSpec(memory_space=pltpu.VMEM), pl.BlockSpec(memory_space=pltpu.HBM)
    dma = pltpu.SemaphoreType.DMA
    grads = [pltpu.VMEM(s, f32) for s in GRADS]
    full = pl.pallas_call(
        functools.partial(kernel, count),
        out_shape=jax.ShapeDtypeStruct((128, 256), f32),
        in_specs=[hbm] * 11,
        out_specs=vmem,
        scratch_shapes=grads + [
            pltpu.VMEM((5, 4, 1024), f32),
            pltpu.VMEM((2, 5, 4, 1024), f32),
            pltpu.VMEM((count, 8, CW), f32),
            pltpu.VMEM((2, 64, 128), f32),
            pltpu.VMEM((2, count, 8, 128), f32),
            pltpu.VMEM((2, 128, 128), f32),
        ] + [dma] * 4 + [dma((2,))] * 5 + [dma] + [dma((6,))],
        compiler_params=pltpu.CompilerParams(
            collective_id=0, has_side_effects=True, vmem_limit_bytes=62 * 1024 * 1024),
    )(initial, forcing, vx, vy, cot, w1.transpose(0, 2, 1), b1.reshape(1, 64), w2,
      b2.reshape(1, 64), w3, b3.reshape(1, 2))
    outs = pl.pallas_call(
        unpack,
        out_shape=[jax.ShapeDtypeStruct(s, f32) for s in GRADS],
        in_specs=[vmem],
        out_specs=[hbm] * 6,
        scratch_shapes=grads + [dma((6,))],
    )(full)
    return (outs[0].transpose(0, 2, 1), outs[1].reshape(64), outs[2], outs[3].reshape(64),
            outs[4], outs[5].reshape(2))


def solution(mesh):
    band, piece = P(("groups", "space"), None), P(("groups", "tm"), "space", None)
    return jax.shard_map(
        functools.partial(per_device, mesh.shape["tm"]),
        mesh=mesh,
        in_specs=(band, piece, band, band, piece) + (P(),) * 6,
        out_specs=(
            P("groups", None, None), P("groups"), P("groups", None, None), P("groups"),
            P("groups", None, None), P("groups"),
        ),
        check_vma=False,
    )
```
